32 devices in a mesh: groups: 2 (over x), expert: 8 (over z, y), dp: 2 (over core).
Axes of the slice: x: 2, y: 2, z: 4, core: 2. Of those that a mesh axis runs over, the one named last changes fastest.
Arguments:
- tokens: bfloat16 [4096, 2048], P(('groups', 'expert', 'dp')), parts along dimension 0, may hold values from -2 to 2
- grad_rows: bfloat16 [4096, 8, 1024], P(('groups', 'expert', 'dp')), parts along dimension 0, may hold values from -2 to 2
- routes: int32 [4096, 8], P(('groups', 'expert', 'dp')), parts along dimension 0, may hold values from 0 to 31, all different within a row; in each aligned block of 128 rows (0 to 127, 128 to 255, ...) at most 96 rows name the same one
- doc_ids: int32 [4096], P(('groups', 'expert', 'dp')), parts along dimension 0, may hold values from 0 to 127, as said below
- input_proj: bfloat16 [32, 64, 2048], P('expert'), may hold values from -0.125 to 0.125
- grad_proj: bfloat16 [32, 64, 1024], P('expert'), may hold values from -0.1875 to 0.1875
Outputs:
- doc_features: float32 [256, 4096], P(('groups', 'expert', 'dp')), parts along dimension 0
The draws below stay inside these ranges and needn't reach their ends.
There are 2 independent parts, one for each index of `groups`. The reference program is written for one: setup_inputs(seed, part) draws one part's arguments, and reference() takes and returns one part's arrays. A program takes and returns all parts, laid end to end along the dimension named above; an argument that names none is the same for every part. Nothing has to cross between parts.
Inputs may be any that keep to these rules, and one draw needn't show every extreme that they name: `routes`: each row names 8 different experts. Within the rows of one device (aligned blocks of 128 tokens) no expert is named more than 96 times, and in every draw some expert is named exactly 96 times by one device. `doc_ids`: ids never fall along the tokens. The tokens of the device with index i along expert+dp (aligned blocks of 128 tokens) belong to documents i * 8 to (i + 1) * 8 - 1, each of which has at least one token.
All inputs are finite; a program needn't handle non-finite values.
Results may differ from the reference program's by a relative error of at most 0.0041.
Values may be sent and summed in bfloat16 or wider, within the bound.
A program may use at most 128 MiB of HBM per device.

```python
import math
import jax
import jax.numpy as jnp
import numpy as np
from jax import lax

D = 2048
FF = 1024
TOP = 8
R = 64
TOK_DEV = 128
DOC_DEV = 8
EXPERTS = 32
CAP = 96
TOKENS = 2048
DOCS = 128


def draw_doc_ids(key, part):
    key = jax.random.fold_in(key, 7)
    blocks = TOKENS // TOK_DEV
    keys = jax.random.split(key, blocks)

    def one_block(block_key):
        shuffled = jax.random.permutation(block_key, TOK_DEV - 1) + 1
        cuts = shuffled[:DOC_DEV - 1]
        places = jnp.arange(TOK_DEV, dtype=jnp.int32)
        return jnp.sum((cuts[None, :] <= places[:, None]).astype(jnp.int32), axis=1)
    local = jax.vmap(one_block)(keys)
    offsets = jnp.arange(blocks, dtype=jnp.int32)[:, None] * DOC_DEV
    return (local + offsets).reshape(-1).astype(jnp.int32)


def shard_levels(stream_key, shape, shards, low, top_value):
    factor_of = 1.0
    for dim, parts in shards:
        draws = jax.random.uniform(jax.random.fold_in(jax.random.fold_in(stream_key, 6), dim), (parts,), jnp.float32, low / len(shards), top_value / len(shards))
        factor_of = factor_of * jnp.repeat(jnp.exp(draws), shape[dim] // parts).reshape((-1,) + (1,) * (len(shape) - 1 - dim))
    return factor_of


def shared_out(key, own, number, rows, number_of, top, bound, lean):
    sequence = jax.random.permutation(key, number_of)
    packed, common = portions_of(number_of, rows * top, bound, lean, True), portions_of(number_of, rows * top, bound, lean, False)
    places = jnp.arange(number_of)

    def named(tallies, offset_by):
        used = int((tallies > 0).sum())
        fixed = max(1, used // 4)
        moved = fixed + (places - fixed + offset_by * (used - fixed)) % max(1, number_of - fixed)
        return jnp.zeros((number_of,), jnp.int32).at[sequence[jnp.where(places < fixed, places, moved)]].set(jnp.asarray(tallies, jnp.int32))

    tallies = jnp.where(number % 4 == 0, named(packed, number // 4), named(common, number - number // 4 - 1))
    mixed = jax.random.permutation(jax.random.fold_in(own, 3), number_of)
    donor, sink = mixed[0:number_of // 2 * 2:2], mixed[1:number_of // 2 * 2:2]
    margin = jnp.minimum(tallies[donor] - 1, bound - tallies[sink]) // 2
    margin = jnp.where((donor == sequence[0]) | (sink == sequence[0]) | (tallies[sink] == 0), 0, jnp.maximum(margin, 0))
    moved = jax.random.randint(jax.random.fold_in(own, 4), (number_of // 2,), 0, 1 << 20) % (margin + 1)
    tallies = tallies.at[donor].add(-moved).at[sink].add(moved)
    labels = jnp.searchsorted(jnp.cumsum(tallies), jnp.arange(rows * top), side="right").astype(jnp.int32)
    listing = labels.reshape(top, rows).T
    listing = listing[jax.random.permutation(jax.random.fold_in(own, 1), rows)]
    offset_by = jax.random.randint(jax.random.fold_in(own, 2), (rows, 1), 0, top)
    return jnp.take_along_axis(listing, (jnp.arange(top)[None, :] + offset_by) % top, axis=1)


def portions_of(count, total, reach, slope, full):
    portions = [(1 << 20) // math.isqrt(grade ** slope) + 1 for grade in range(1, count + 1)]
    largest = reach if full else min(reach, max(-(-total // count), total * portions[0] // sum(portions)))
    least = 1 if total - largest >= count - 1 else 0
    counts, rest = [largest] + [least] * (count - 1), total - largest - least * (count - 1)
    while rest > 0:
        candidates = [i for i in range(1, count) if counts[i] < largest] or [i for i in range(1, count) if counts[i] < reach]
        mass, left = sum([portions[i] for i in candidates]), rest
        for i in candidates:
            extra = min(reach - counts[i], max(1, left * portions[i] // mass), rest)
            counts[i] = counts[i] + extra
            rest = rest - extra
    return np.array(counts)


def noise(rng, extent, deviation, most, shards=(), kind=jnp.bfloat16):
    level = shard_levels(rng, extent, shards, -0.22, 0.18) if shards else 1.0
    entries = jax.random.normal(rng, extent, jnp.float32) * deviation * level
    return jnp.minimum(jnp.maximum(entries, -most), most).astype(kind)


def setup_inputs(seed: int = 0, part: int = 0) -> dict:
    key_of = jax.random.split(jax.random.key(seed), 7)
    own_keys = jax.random.split(jax.random.fold_in(key_of[6], part), 7)
    tokens = noise(own_keys[0], (TOKENS, D), 0.25, 2.0, ((0, 16),))
    grad_rows = noise(own_keys[1], (TOKENS, TOP, FF), 0.25, 2.0, ((0, 16),))
    routes_keys = jax.random.split(jax.random.fold_in(own_keys[2], 1), TOKENS // TOK_DEV)
    routes_turns = jax.random.permutation(jax.random.fold_in(own_keys[2], 3), TOKENS // TOK_DEV)
    routes = jax.vmap(lambda own, number: shared_out(jax.random.fold_in(own_keys[2], 2), own, number, TOK_DEV, EXPERTS, TOP, CAP, 2))(routes_keys, routes_turns).reshape((TOKENS, TOP))
    doc_ids = draw_doc_ids(jax.random.fold_in(jax.random.fold_in(key_of[6], part), 71), part)
    input_proj = noise(key_of[4], (EXPERTS, R, D), D ** -0.5, 0.125, ((0, 8),))
    grad_proj = noise(key_of[5], (EXPERTS, R, FF), FF ** -0.5, 0.1875, ((0, 8),))
    return {"tokens": tokens, "grad_rows": grad_rows, "routes": routes, "doc_ids": doc_ids, "input_proj": input_proj, "grad_proj": grad_proj}


def reference(tokens, grad_rows, routes, doc_ids, input_proj, grad_proj):
    fanout = routes.shape[1]
    proj_rank = input_proj.shape[1]
    tok_block = math.gcd(TOK_DEV, 32)
    turns = TOKENS // tok_block

    def one_block(totals, index):
        first = index * tok_block
        tok_part = lax.dynamic_slice_in_dim(tokens, first, tok_block, 0).astype(jnp.float32)
        grad_part = lax.dynamic_slice_in_dim(grad_rows, first, tok_block, 0).astype(jnp.float32)
        route_part = lax.dynamic_slice_in_dim(routes, first, tok_block, 0)
        doc_part = lax.dynamic_slice_in_dim(doc_ids, first, tok_block, 0)
        in_mats = input_proj[route_part].astype(jnp.float32)
        grad_mats = grad_proj[route_part].astype(jnp.float32)
        feat_in = jnp.einsum("bkrd,bd->bkr", in_mats, tok_part)
        feat_in = lax.optimization_barrier(feat_in.astype(jnp.bfloat16)).astype(jnp.float32)
        feat_grad = jnp.einsum("bkrf,bkf->bkr", grad_mats, grad_part)
        feat_grad = lax.optimization_barrier(feat_grad.astype(jnp.bfloat16)).astype(jnp.float32)
        outer = (feat_grad[:, :, :, None] * feat_in[:, :, None, :]).reshape(tok_block * fanout, proj_rank * proj_rank)
        pair_docs = jnp.repeat(doc_part, fanout)
        return totals + jax.ops.segment_sum(outer, pair_docs, num_segments=DOCS), None

    start_totals = jnp.zeros((DOCS, proj_rank * proj_rank), jnp.float32)
    totals, _ = lax.scan(one_block, start_totals, jnp.arange(turns, dtype=jnp.int32))
    return totals
```

```python
import jax
import jax.numpy as jnp
from jax import lax
from jax.sharding import PartitionSpec as P

DOC_DEV = 8


def shards(tokens, grad_rows, routes, doc_ids, input_proj, grad_proj):
    tok, fan = routes.shape
    rank = input_proj.shape[1]
    local = input_proj.shape[0]
    experts = local * lax.axis_size("expert")
    core = lax.axis_index("dp")
    half = local // lax.axis_size("dp")

    def gather(w):
        mine = lax.dynamic_slice_in_dim(w, core * half, half, 0)
        part = lax.all_gather(mine, "expert", axis=0)
        both = lax.all_gather(part, "dp", axis=1)
        return both.reshape((experts * rank, w.shape[2]))

    w_in = gather(input_proj)
    w_gr = gather(grad_proj)
    dense_in = jnp.einsum("td,nd->tn", tokens, w_in, preferred_element_type=jnp.float32)
    dense_in = dense_in.astype(jnp.bfloat16).reshape(tok, experts, rank)
    flat = grad_rows.reshape(tok * fan, grad_rows.shape[2])
    dense_gr = jnp.einsum("pf,nf->pn", flat, w_gr, preferred_element_type=jnp.float32)
    dense_gr = dense_gr.reshape(tok, fan, experts, rank)
    pick = routes[:, :, None] == jnp.arange(experts, dtype=jnp.int32)
    feat_gr = jnp.sum(jnp.where(pick[..., None], dense_gr, 0.0), axis=2).astype(jnp.bfloat16)
    feat_in = jnp.einsum("tke,ter->tkr", pick.astype(jnp.bfloat16), dense_in,
                         preferred_element_type=jnp.float32).astype(jnp.bfloat16)
    first = (lax.axis_index("expert") * lax.axis_size("dp") + core) * DOC_DEV
    marks = ((doc_ids - first)[:, None] == jnp.arange(DOC_DEV, dtype=jnp.int32)).astype(jnp.bfloat16)
    left = marks[:, None, :, None] * feat_gr[:, :, None, :]
    out = lax.dot_general(left.reshape(tok * fan, DOC_DEV * rank), feat_in.reshape(tok * fan, rank),
                          (((0,), (0,)), ((), ())), preferred_element_type=jnp.float32)
    return out.reshape(DOC_DEV, rank * rank)


def solution(mesh):
    in_specs = (
        P(("groups", "expert", "dp"), None),
        P(("groups", "expert", "dp"), None, None),
        P(("groups", "expert", "dp"), None),
        P(("groups", "expert", "dp")),
        P("expert", None, None),
        P("expert", None, None),
    )
    out_specs = P(("groups", "expert", "dp"), None)
    return jax.shard_map(shards, mesh=mesh, in_specs=in_specs, out_specs=out_specs, check_vma=False)
```

```python
import functools

import jax
import jax.numpy as jnp
from jax import lax
from jax.experimental import pallas as pl
from jax.experimental.pallas import tpu as pltpu
from jax.sharding import PartitionSpec as P

DOC_DEV = 8
MESH = pl.DeviceIdType.MESH
LO, HI, XP, CORE, YP = range(5)
NT = (((1,), (1,)), ((), ()))
FULL_IN = (1,)


def kernel(zn, yn, tok_hbm, grad_hbm, routes_ref, doc_ref, win_hbm, wgr_hbm, out_ref,
           tok, grads, win, wgr, feat_send, feat_recv, acc_in, acc_gr, route_at,
           local_sem, in_recv, gr_recv, in_send, gr_send,
           tok_send_sem, tok_recv_sem, feat_send_sem, feat_recv_sem):
    group = lax.axis_index("groups")
    place = lax.axis_index("expert")
    core = lax.axis_index("dp")
    z, y = place // yn, place % yn
    hx = group % 2
    tokens = tok_hbm.shape[0]
    pairs = grad_hbm.shape[0]
    cols = win.shape[1]
    part = cols // 4
    last = zn - 1
    to = {
        LO: {"expert": place - yn},
        HI: {"expert": place + yn},
        XP: {"groups": group + 1 - 2 * hx},
        CORE: {"dp": 1 - core},
    }
    if yn == 2:
        to[YP] = {"expert": place + 1 - 2 * y}

    def have(link):
        if link == LO:
            return z > 0
        if link == HI:
            return z < last
        return None

    def when(conds, fn):
        conds = [c for c in conds if c is not None]
        if not conds:
            fn()
            return
        both = conds[0]
        for c in conds[1:]:
            both = jnp.logical_and(both, c)
        pl.when(both)(fn)

    def valid(d, sign):
        if d == 0:
            return None
        return z + d <= last if sign > 0 else z - d >= 0

    slot_own = z * yn + y
    local = [
        pltpu.make_async_copy(tok_hbm, tok.at[pl.ds(0, tokens)], local_sem.at[0]),
        pltpu.make_async_copy(wgr_hbm, wgr.at[slot_own], local_sem.at[1]),
        pltpu.make_async_copy(grad_hbm, grads, local_sem.at[2]),
        pltpu.make_async_copy(win_hbm, win.at[z], local_sem.at[3]),
    ]
    for c in local:
        c.start()

    barrier = pltpu.get_barrier_semaphore()
    for link in to:
        def greet(link=link):
            pl.semaphore_signal(barrier, inc=1, device_id=to[link], device_id_type=MESH)
        when([have(link)], greet)
    inner = (z > 0).astype(jnp.int32) + (z < last).astype(jnp.int32)
    pl.semaphore_wait(barrier, len(to) - 2 + inner)

    sent = []

    def send(make, conds):
        when(conds, lambda: make().start())
        sent.append((make, conds))

    def rows_of(dh, dc=0):
        half = hx if dh == 0 else 1 - hx
        which = core if dc == 0 else 1 - core
        return pl.ds(pl.multiple_of((half * 2 + which) * part, part), part), half * 2 + which

    def pack(kind, d, sign, yr):
        zz = z + sign * d
        if kind == "in":
            return win, zz, in_send, in_recv
        yy = y if yr == 0 else 1 - y
        return wgr, zz * yn + yy, gr_send, gr_recv

    def send_piece(kind, d, sign, yr, dh, link):
        buf, slot, ssem, rsem = pack(kind, d, sign, yr)
        rows, number = rows_of(dh)
        if d == 0 and yr == 0:
            src = (win_hbm if kind == "in" else wgr_hbm).at[rows]
        else:
            src = buf.at[slot, rows]

        def make():
            return pltpu.make_async_remote_copy(
                src_ref=src, dst_ref=buf.at[slot, rows],
                send_sem=ssem.at[link, slot, dh], recv_sem=rsem.at[slot, number],
                device_id=to[link], device_id_type=MESH)
        send(make, [valid(d, sign), have(link)])

    def arrive(kind, d, sign, yr, dh, dc=0):
        buf, slot, ssem, rsem = pack(kind, d, sign, yr)
        rows, number = rows_of(dh, dc)

        def wait():
            pltpu.make_async_remote_copy(
                src_ref=buf.at[slot, rows], dst_ref=buf.at[slot, rows],
                send_sem=ssem.at[CORE, slot, dh], recv_sem=rsem.at[slot, number],
                device_id=to[CORE], device_id_type=MESH).wait_recv()
        when([valid(d, sign)], wait)

    def z_event(kind, d, sign):
        link = LO if sign > 0 else HI
        arrive(kind, d, sign, 0, 0)
        if d < last:
            send_piece(kind, d, sign, 0, 0, link)
        full = kind == "in" and d in FULL_IN
        if kind == "gr" and yn == 2:
            send_piece(kind, d, sign, 0, 0, YP)
        if not full:
            send_piece(kind, d, sign, 0, 0, XP)
        send_piece(kind, d, sign, 0, 0, CORE)
        if full:
            arrive(kind, d, sign, 0, 1)
            if d < last and d + 1 in FULL_IN:
                send_piece(kind, d, sign, 0, 1, link)
            send_piece(kind, d, sign, 0, 1, CORE)

    def y_event(d, sign):
        arrive("gr", d, sign, 1, 0)
        if d > 0:
            send_piece("gr", d, sign, 1, 0, XP)
        send_piece("gr", d, sign, 1, 0, CORE)
        if d == 0:
            arrive("gr", d, sign, 1, 1)
            send_piece("gr", d, sign, 1, 1, CORE)

    def x_event(kind, d, sign, yr):
        if kind == "in" and d in FULL_IN:
            return
        arrive(kind, d, sign, yr, 1)
        if kind == "in" and d < last and d + 1 in FULL_IN:
            send_piece(kind, d, sign, yr, 1, LO if sign > 0 else HI)
        send_piece(kind, d, sign, yr, 1, CORE)

    def core_event(kind, d, sign, yr):
        arrive(kind, d, sign, yr, 0, 1)
        arrive(kind, d, sign, yr, 1, 1)

    tile = 256

    def select(acc, at, slot, value):
        hit = route_at[pl.ds(at, tile), :]
        acc[pl.ds(at, tile), :] = jnp.where(
            hit == 4 * slot, value[:, :128],
            jnp.where(hit == 4 * slot + 2, value[:, 128:], acc[pl.ds(at, tile), :]))

    def project_grads(d, sign, yr):
        _, slot, _, _ = pack("gr", d, sign, yr)

        def run():
            @pl.loop(0, pairs // tile)
            def _(i):
                at = pl.multiple_of(i * tile, tile)
                value = lax.dot_general(grads[pl.ds(at, tile), :], wgr[slot], NT,
                                        preferred_element_type=jnp.float32)
                select(acc_gr, at, slot, value)
        when([valid(d, sign)], run)

    fan = pairs // tokens

    def select_inputs(slot, block):
        @pl.loop(0, pairs // tile)
        def _(i):
            at = pl.multiple_of(i * tile, tile)
            few = tile // fan
            value = block[pl.ds(pl.multiple_of(i * few, few), few), :].astype(jnp.float32)
            value = jnp.broadcast_to(value[:, None, :], (few, fan, cols)).reshape(tile, cols)
            select(acc_in, at, slot, value)

    def project_inputs(d, sign):
        _, slot, _, _ = pack("in", d, sign, 0)

        def run():
            value = lax.dot_general(tok[...], win[slot], NT, preferred_element_type=jnp.float32)
            feat_send[slot] = value.astype(jnp.bfloat16)
        when([valid(d, sign)], run)
        if yn == 2:
            def make():
                return pltpu.make_async_remote_copy(
                    src_ref=feat_send.at[slot, pl.ds(tokens, tokens)], dst_ref=feat_recv.at[slot],
                    send_sem=feat_send_sem.at[slot], recv_sem=feat_recv_sem.at[slot],
                    device_id=to[YP], device_id_type=MESH)
            send(make, [valid(d, sign)])
        when([valid(d, sign)], lambda: select_inputs(slot * yn + y, feat_send.at[slot]))

    def features_back(d, sign):
        if yn == 1:
            return
        _, slot, _, _ = pack("in", d, sign, 0)

        def run():
            pltpu.make_async_remote_copy(
                src_ref=feat_recv.at[slot], dst_ref=feat_recv.at[slot],
                send_sem=feat_send_sem.at[slot], recv_sem=feat_recv_sem.at[slot],
                device_id=to[YP], device_id_type=MESH).wait_recv()
            select_inputs(slot * yn + 1 - y, feat_recv.at[slot])
        when([valid(d, sign)], run)

    for link in (LO, HI):
        send_piece("gr", 0, 1, 0, 0, link)
        send_piece("in", 0, 1, 0, 0, link)
        if 1 in FULL_IN:
            send_piece("in", 0, 1, 0, 1, link)
    if yn == 2:
        def make_tok():
            return pltpu.make_async_remote_copy(
                src_ref=tok_hbm, dst_ref=tok.at[pl.ds(tokens, tokens)],
                send_sem=tok_send_sem, recv_sem=tok_recv_sem,
                device_id=to[YP], device_id_type=MESH)
        send(make_tok, [])
        send_piece("gr", 0, 1, 0, 0, YP)
        send_piece("gr", 0, 1, 0, 1, YP)

    pair = lax.broadcasted_iota(jnp.int32, (pairs, tokens), 0) // fan
    spread = (pair == lax.broadcasted_iota(jnp.int32, (pairs, tokens), 1)).astype(jnp.bfloat16)
    named = jnp.dot(spread, routes_ref[...].astype(jnp.bfloat16), preferred_element_type=jnp.float32)
    choice = lax.broadcasted_iota(jnp.int32, (pairs, fan), 0) % fan
    mine = choice == lax.broadcasted_iota(jnp.int32, (pairs, fan), 1)
    named = jnp.sum(jnp.where(mine, named, 0.0), axis=1, keepdims=True).astype(jnp.int32)
    half_of = lax.broadcasted_iota(jnp.int32, (pairs, 128), 1) // 64
    route_at[...] = named - half_of
    acc_in[...] = jnp.zeros_like(acc_in)
    acc_gr[...] = jnp.zeros_like(acc_gr)
    for c in local:
        c.wait()

    signs = (1, -1)
    other = tuple(range(1, yn))
    project_grads(0, 1, 0)
    for d in range(1, zn):
        for s in signs:
            z_event("gr", d, s)
        if d > 1:
            for s in signs:
                x_event("in", d - 1, s, 0)
        for s in signs:
            z_event("in", d, s)
        if d == 1:
            if yn == 2:
                make_tok().wait_recv()
            project_inputs(0, 1)
            if yn == 2:
                y_event(0, 1)
                core_event("gr", 0, 1, 1)
                project_grads(0, 1, 1)
            features_back(0, 1)
        for s in signs:
            x_event("gr", d, s, 0)
        for e in other:
            for s in signs:
                y_event(d, s)
        if d > 1:
            for s in signs:
                core_event("in", d - 1, s, 0)
                project_inputs(d - 1, s)
            for s in signs:
                core_event("gr", d - 1, s, 0)
                project_grads(d - 1, s, 0)
            for e in other:
                for s in signs:
                    x_event("gr", d - 1, s, e)
            for e in other:
                for s in signs:
                    core_event("gr", d - 1, s, e)
                    project_grads(d - 1, s, e)
            for s in signs:
                features_back(d - 1, s)
    for s in signs:
        x_event("in", last, s, 0)
    for e in other:
        for s in signs:
            x_event("gr", last, s, e)
    for s in signs:
        core_event("gr", last, s, 0)
        project_grads(last, s, 0)
    for s in signs:
        core_event("in", last, s, 0)
        project_inputs(last, s)
    for e in other:
        for s in signs:
            core_event("gr", last, s, e)
            project_grads(last, s, e)
    for s in signs:
        features_back(last, s)

    right = acc_in[...]
    right = (right + pltpu.roll(right, 64, 1)).astype(jnp.bfloat16)
    left = acc_gr[...]
    left = (left + pltpu.roll(left, 64, 1)).astype(jnp.bfloat16).astype(jnp.float32)
    left = left.T
    docs = out_ref.shape[0]
    first = (place * lax.axis_size("dp") + core) * docs
    own_doc = jnp.broadcast_to(doc_ref[...] - first, (docs, tokens)).astype(jnp.bfloat16)
    pair = lax.broadcasted_iota(jnp.int32, (tokens, pairs), 1) // fan
    spread = (pair == lax.broadcasted_iota(jnp.int32, (tokens, pairs), 0)).astype(jnp.bfloat16)
    pair_doc = jnp.dot(own_doc, spread, preferred_element_type=jnp.float32).astype(jnp.int32)
    marks = pair_doc == lax.broadcasted_iota(jnp.int32, (docs, pairs), 0)
    low = lax.broadcasted_iota(jnp.int32, (docs, 128), 1) < 64
    step = 16
    for a in range(0, 64, step):
        block = jnp.broadcast_to(left[a:a + step][:, None, :], (step, docs, pairs))
        block = jnp.where(marks[None], block, 0.0).reshape(step * docs, pairs)
        got = jnp.dot(block.astype(jnp.bfloat16), right, preferred_element_type=jnp.float32)
        for j in range(0, step, 2):
            at = (a + j) * 64
            out_ref[:, at:at + 128] = jnp.where(
                low, got[j * docs:(j + 1) * docs], got[(j + 1) * docs:(j + 2) * docs])

    for make, conds in sent:
        when(conds, lambda: make().wait_send())


def shards(yn, tokens, grad_rows, routes, doc_ids, input_proj, grad_proj):
    tok, fan = routes.shape
    local, rank, width = input_proj.shape
    hidden = grad_proj.shape[2]
    zn = lax.axis_size("expert") // yn
    cols = local * rank
    pairs = tok * fan
    vmem = pl.BlockSpec(memory_space=pltpu.VMEM)
    hbm = pl.BlockSpec(memory_space=pl.ANY)
    dma = pltpu.SemaphoreType.DMA
    return pl.pallas_call(
        functools.partial(kernel, zn, yn),
        out_shape=jax.ShapeDtypeStruct((DOC_DEV, rank * rank), jnp.float32),
        in_specs=[hbm, hbm, vmem, vmem, hbm, hbm],
        out_specs=vmem,
        scratch_shapes=[
            pltpu.VMEM((yn * tok, width), jnp.bfloat16),
            pltpu.VMEM((pairs, hidden), jnp.bfloat16),
            pltpu.VMEM((zn, cols, width), jnp.bfloat16),
            pltpu.VMEM((zn * yn, cols, hidden), jnp.bfloat16),
            pltpu.VMEM((zn, yn * tok, cols), jnp.bfloat16),
            pltpu.VMEM((zn, tok, cols), jnp.bfloat16),
            pltpu.VMEM((pairs, 128), jnp.float32),
            pltpu.VMEM((pairs, 128), jnp.float32),
            pltpu.VMEM((pairs, 128), jnp.int32),
            dma((4,)),
            dma((zn, 4)),
            dma((zn * yn, 4)),
            dma((4, zn, 2)),
            dma((5, zn * yn, 2)),
            dma,
            dma,
            dma((zn,)),
            dma((zn,)),
        ],
        compiler_params=pltpu.CompilerParams(
            collective_id=0, has_side_effects=True, vmem_limit_bytes=56 * 2**20),
        cost_estimate=pl.CostEstimate(
            flops=2 * pairs * hidden * cols * zn * yn + 2 * tok * yn * width * cols * zn,
            bytes_accessed=16 * 2**20, transcendentals=0),
        name="project_and_sum",
    )(tokens, grad_rows.reshape(pairs, hidden), routes, doc_ids.reshape(1, tok),
      input_proj.reshape(cols, width), grad_proj.reshape(cols, hidden))


def solution(mesh):
    in_specs = (
        P(("groups", "expert", "dp"), None),
        P(("groups", "expert", "dp"), None, None),
        P(("groups", "expert", "dp"), None),
        P(("groups", "expert", "dp")),
        P("expert", None, None),
        P("expert", None, None),
    )
    out_specs = P(("groups", "expert", "dp"), None)
    yn = 2 if mesh.shape["expert"] == 8 else 1
    return jax.shard_map(functools.partial(shards, yn), mesh=mesh, in_specs=in_specs,
                         out_specs=out_specs, check_vma=False)
```

```python
import functools

import jax
import jax.numpy as jnp
from jax import lax
from jax.experimental import pallas as pl
from jax.experimental.pallas import tpu as pltpu
from jax.sharding import PartitionSpec as P

DOC_DEV = 8
MESH = pl.DeviceIdType.MESH
LO, HI, XP, CORE, YP = range(5)
NT = (((1,), (1,)), ((), ()))
FULL_IN = (3,)
FULL_GR = (1,)
FULL_Y = (0, 1)
FIRST_Z = ("in", "gr")
FIRST_Y = ("gr", "tok")


def order_of(zn, yn):
    if (zn, yn) == (4, 2):
        return ORDER
    order = [("K", "gr", 0, 1, 0), ("T", 0, 1)]
    if yn == 2:
        order += [("Y", 0, 1), ("K", "gr", 0, 1, 1)]
    for d in range(1, zn):
        for s in (1, -1):
            order += [("Z", "gr", d, s), ("Z", "in", d, s)]
        for s in (1, -1):
            order += [("X", "gr", d, s, 0), ("X", "in", d, s, 0)]
            if yn == 2:
                order += [("Y", d, s), ("X", "gr", d, s, 1)]
        for s in (1, -1):
            order += [("K", "gr", d, s, 0), ("K", "in", d, s, 0)]
            if yn == 2:
                order += [("K", "gr", d, s, 1)]
    if yn == 2:
        order += [("F", d, s) for d in range(zn) for s in ((1, -1) if d else (1,))]
    return order


ORDER = [
    ("Y", 0, 1), ("X", "gr", 1, 1, 1), ("Z", "in", 1, 1), ("Z", "gr", 1, -1), ("Z", "in", 1, -1),
    ("Z", "gr", 2, -1), ("K", "gr", 1, -1, 0), ("Z", "gr", 1, 1), ("X", "in", 3, -1, 0),
    ("K", "gr", 0, 1, 1), ("X", "in", 1, 1, 0), ("X", "in", 3, 1, 0), ("Z", "in", 2, 1),
    ("X", "gr", 2, -1, 0), ("Z", "gr", 2, 1), ("Z", "in", 2, -1), ("T", 0, 1), ("Y", 1, -1),
    ("K", "in", 1, 1, 0), ("K", "gr", 1, -1, 1), ("X", "in", 2, 1, 0), ("X", "gr", 1, -1, 0),
    ("K", "gr", 2, -1, 0), ("Y", 2, -1), ("X", "in", 2, -1, 0), ("Z", "gr", 3, -1),
    ("X", "in", 1, -1, 0), ("K", "gr", 0, 1, 0), ("X", "gr", 2, -1, 1), ("K", "in", 2, -1, 0),
    ("K", "gr", 1, 1, 0), ("Y", 2, 1), ("Z", "gr", 3, 1), ("Y", 3, -1), ("Y", 1, 1),
    ("K", "in", 1, -1, 0), ("F", 0, 1), ("K", "in", 2, 1, 0), ("Z", "in", 3, -1), ("F", 2, -1),
    ("X", "gr", 3, -1, 0), ("K", "gr", 2, -1, 1), ("X", "gr", 2, 1, 1), ("K", "gr", 1, 1, 1),
    ("F", 1, -1), ("Y", 3, 1), ("K", "in", 3, -1, 0), ("K", "gr", 2, 1, 1), ("Z", "in", 3, 1),
    ("F", 1, 1), ("X", "gr", 1, 1, 0), ("X", "gr", 3, -1, 1), ("X", "gr", 1, -1, 1),
    ("K", "gr", 3, -1, 0), ("X", "gr", 2, 1, 0), ("K", "gr", 3, -1, 1), ("X", "gr", 3, 1, 0),
    ("F", 2, 1), ("K", "in", 3, 1, 0), ("K", "gr", 2, 1, 0), ("X", "gr", 3, 1, 1),
    ("K", "gr", 3, 1, 0), ("K", "gr", 3, 1, 1), ("F", 3, 1), ("F", 3, -1),
]


def kernel(zn, yn, order, tok_hbm, grad_hbm, routes_ref, doc_ref, win_hbm, wgr_hbm, out_ref,
           tok, grads, win, wgr, feat_send, feat_recv, acc_in, acc_gr, route_at,
           local_sem, in_recv, gr_recv, in_send, gr_send,
           tok_send_sem, tok_recv_sem, feat_send_sem, feat_recv_sem):
    group = lax.axis_index("groups")
    place = lax.axis_index("expert")
    core = lax.axis_index("dp")
    z, y = place // yn, place % yn
    hx = group % 2
    tokens = tok_hbm.shape[0]
    pairs = grad_hbm.shape[0]
    cols = win.shape[1]
    part = cols // 4
    last = zn - 1
    to = {
        LO: {"expert": place - yn},
        HI: {"expert": place + yn},
        XP: {"groups": group + 1 - 2 * hx},
        CORE: {"dp": 1 - core},
    }
    if yn == 2:
        to[YP] = {"expert": place + 1 - 2 * y}

    def have(link):
        if link == LO:
            return z > 0
        if link == HI:
            return z < last
        return None

    def when(conds, fn):
        conds = [c for c in conds if c is not None]
        if not conds:
            fn()
            return
        both = conds[0]
        for c in conds[1:]:
            both = jnp.logical_and(both, c)
        pl.when(both)(fn)

    def valid(d, sign):
        if d == 0:
            return None
        return z + d <= last if sign > 0 else z - d >= 0

    slot_own = z * yn + y
    local = [
        pltpu.make_async_copy(tok_hbm, tok.at[pl.ds(0, tokens)], local_sem.at[0]),
        pltpu.make_async_copy(wgr_hbm, wgr.at[slot_own], local_sem.at[1]),
        pltpu.make_async_copy(grad_hbm, grads, local_sem.at[2]),
        pltpu.make_async_copy(win_hbm, win.at[z], local_sem.at[3]),
    ]
    for c in local:
        c.start()

    barrier = pltpu.get_barrier_semaphore()
    for link in to:
        def greet(link=link):
            pl.semaphore_signal(barrier, inc=1, device_id=to[link], device_id_type=MESH)
        when([have(link)], greet)
    inner = (z > 0).astype(jnp.int32) + (z < last).astype(jnp.int32)
    pl.semaphore_wait(barrier, len(to) - 2 + inner)

    sent = []

    def send(make, conds):
        when(conds, lambda: make().start())
        sent.append((make, conds))

    def rows_of(dh, dc=0):
        half = hx if dh == 0 else 1 - hx
        which = core if dc == 0 else 1 - core
        return pl.ds(pl.multiple_of((half * 2 + which) * part, part), part), half * 2 + which

    def pack(kind, d, sign, yr):
        zz = z + sign * d
        if kind == "in":
            return win, zz, in_send, in_recv
        yy = y if yr == 0 else 1 - y
        return wgr, zz * yn + yy, gr_send, gr_recv

    def send_piece(kind, d, sign, yr, dh, link):
        buf, slot, ssem, rsem = pack(kind, d, sign, yr)
        rows, number = rows_of(dh)
        if d == 0 and yr == 0:
            src = (win_hbm if kind == "in" else wgr_hbm).at[rows]
        else:
            src = buf.at[slot, rows]

        def make():
            return pltpu.make_async_remote_copy(
                src_ref=src, dst_ref=buf.at[slot, rows],
                send_sem=ssem.at[link, slot, dh], recv_sem=rsem.at[slot, number],
                device_id=to[link], device_id_type=MESH)
        send(make, [valid(d, sign), have(link)])

    def arrive(kind, d, sign, yr, dh, dc=0):
        buf, slot, ssem, rsem = pack(kind, d, sign, yr)
        rows, number = rows_of(dh, dc)

        def wait():
            pltpu.make_async_remote_copy(
                src_ref=buf.at[slot, rows], dst_ref=buf.at[slot, rows],
                send_sem=ssem.at[CORE, slot, dh], recv_sem=rsem.at[slot, number],
                device_id=to[CORE], device_id_type=MESH).wait_recv()
        when([valid(d, sign)], wait)

    full_z = {"in": FULL_IN, "gr": FULL_GR}

    def z_event(kind, d, sign):
        link = LO if sign > 0 else HI
        full = d in full_z[kind]
        arrive(kind, d, sign, 0, 0)
        if d < last:
            send_piece(kind, d, sign, 0, 0, link)
        if kind == "gr" and yn == 2:
            send_piece(kind, d, sign, 0, 0, YP)
        if not full:
            send_piece(kind, d, sign, 0, 0, XP)
        send_piece(kind, d, sign, 0, 0, CORE)
        if full:
            arrive(kind, d, sign, 0, 1)
            other_half(kind, d, sign)

    def other_half(kind, d, sign):
        if d < last and d + 1 in full_z[kind]:
            send_piece(kind, d, sign, 0, 1, LO if sign > 0 else HI)
        if kind == "gr" and yn == 2 and d in FULL_Y:
            send_piece(kind, d, sign, 0, 1, YP)
        send_piece(kind, d, sign, 0, 1, CORE)

    def y_event(d, sign):
        arrive("gr", d, sign, 1, 0)
        if d not in FULL_Y:
            send_piece("gr", d, sign, 1, 0, XP)
        send_piece("gr", d, sign, 1, 0, CORE)
        if d in FULL_Y:
            arrive("gr", d, sign, 1, 1)
            send_piece("gr", d, sign, 1, 1, CORE)

    def x_event(kind, d, sign, yr):
        if d in (full_z[kind] if yr == 0 else FULL_Y):
            return
        arrive(kind, d, sign, yr, 1)
        if yr == 0:
            other_half(kind, d, sign)
        else:
            send_piece(kind, d, sign, yr, 1, CORE)

    def core_event(kind, d, sign, yr):
        arrive(kind, d, sign, yr, 0, 1)
        arrive(kind, d, sign, yr, 1, 1)

    tile = 256

    def select(acc, at, slot, value):
        hit = route_at[pl.ds(at, tile), :]
        acc[pl.ds(at, tile), :] = jnp.where(
            hit == 4 * slot, value[:, :128],
            jnp.where(hit == 4 * slot + 2, value[:, 128:], acc[pl.ds(at, tile), :]))

    def project_grads(d, sign, yr):
        _, slot, _, _ = pack("gr", d, sign, yr)

        def run():
            @pl.loop(0, pairs // tile)
            def _(i):
                at = pl.multiple_of(i * tile, tile)
                value = lax.dot_general(grads[pl.ds(at, tile), :], wgr[slot], NT,
                                        preferred_element_type=jnp.float32)
                select(acc_gr, at, slot, value)
        when([valid(d, sign)], run)

    fan = pairs // tokens

    def select_inputs(slot, block):
        @pl.loop(0, pairs // tile)
        def _(i):
            at = pl.multiple_of(i * tile, tile)
            few = tile // fan
            value = block[pl.ds(pl.multiple_of(i * few, few), few), :].astype(jnp.float32)
            value = jnp.broadcast_to(value[:, None, :], (few, fan, cols)).reshape(tile, cols)
            select(acc_in, at, slot, value)

    def project_inputs(d, sign):
        _, slot, _, _ = pack("in", d, sign, 0)

        def run():
            value = lax.dot_general(tok[...], win[slot], NT, preferred_element_type=jnp.float32)
            feat_send[slot] = value.astype(jnp.bfloat16)
        when([valid(d, sign)], run)
        if yn == 2:
            def make():
                return pltpu.make_async_remote_copy(
                    src_ref=feat_send.at[slot, pl.ds(tokens, tokens)], dst_ref=feat_recv.at[slot],
                    send_sem=feat_send_sem.at[slot], recv_sem=feat_recv_sem.at[slot],
                    device_id=to[YP], device_id_type=MESH)
            send(make, [valid(d, sign)])
        when([valid(d, sign)], lambda: select_inputs(slot * yn + y, feat_send.at[slot]))

    def features_back(d, sign):
        if yn == 1:
            return
        _, slot, _, _ = pack("in", d, sign, 0)

        def run():
            pltpu.make_async_remote_copy(
                src_ref=feat_recv.at[slot], dst_ref=feat_recv.at[slot],
                send_sem=feat_send_sem.at[slot], recv_sem=feat_recv_sem.at[slot],
                device_id=to[YP], device_id_type=MESH).wait_recv()
            select_inputs(slot * yn + 1 - y, feat_recv.at[slot])
        when([valid(d, sign)], run)

    def make_tok():
        return pltpu.make_async_remote_copy(
            src_ref=tok_hbm, dst_ref=tok.at[pl.ds(tokens, tokens)],
            send_sem=tok_send_sem, recv_sem=tok_recv_sem,
            device_id=to[YP], device_id_type=MESH)

    for kind in FIRST_Z:
        for link in (LO, HI):
            send_piece(kind, 0, 1, 0, 0, link)
            if 1 in full_z[kind]:
                send_piece(kind, 0, 1, 0, 1, link)
    if yn == 2:
        for what in FIRST_Y:
            if what == "tok":
                send(make_tok, [])
                continue
            send_piece("gr", 0, 1, 0, 0, YP)
            if 0 in FULL_Y:
                send_piece("gr", 0, 1, 0, 1, YP)

    pair = lax.broadcasted_iota(jnp.int32, (pairs, tokens), 0) // fan
    spread = (pair == lax.broadcasted_iota(jnp.int32, (pairs, tokens), 1)).astype(jnp.bfloat16)
    named = jnp.dot(spread, routes_ref[...].astype(jnp.bfloat16), preferred_element_type=jnp.float32)
    choice = lax.broadcasted_iota(jnp.int32, (pairs, fan), 0) % fan
    mine = choice == lax.broadcasted_iota(jnp.int32, (pairs, fan), 1)
    named = jnp.sum(jnp.where(mine, named, 0.0), axis=1, keepdims=True).astype(jnp.int32)
    half_of = lax.broadcasted_iota(jnp.int32, (pairs, 128), 1) // 64
    route_at[...] = named - half_of
    acc_in[...] = jnp.zeros_like(acc_in)
    acc_gr[...] = jnp.zeros_like(acc_gr)
    for c in local:
        c.wait()

    def run_event(event):
        what = event[0]
        if what == "Z":
            z_event(*event[1:])
        elif what == "X":
            x_event(*event[1:])
        elif what == "Y":
            y_event(*event[1:])
        elif what == "F":
            features_back(*event[1:])
        elif what == "T":
            if yn == 2:
                make_tok().wait_recv()
            project_inputs(0, 1)
        else:
            kind, d, sign, yr = event[1:]
            if (d, yr) != (0, 0):
                core_event(kind, d, sign, yr)
            if kind == "in":
                project_inputs(d, sign)
            else:
                project_grads(d, sign, yr)

    for event in order:
        run_event(event)

    right = acc_in[...]
    right = (right + pltpu.roll(right, 64, 1)).astype(jnp.bfloat16)
    left = acc_gr[...]
    left = (left + pltpu.roll(left, 64, 1)).astype(jnp.bfloat16).astype(jnp.float32)
    left = left.T
    docs = out_ref.shape[0]
    first = (place * lax.axis_size("dp") + core) * docs
    own_doc = jnp.broadcast_to(doc_ref[...] - first, (docs, tokens)).astype(jnp.bfloat16)
    pair = lax.broadcasted_iota(jnp.int32, (tokens, pairs), 1) // fan
    spread = (pair == lax.broadcasted_iota(jnp.int32, (tokens, pairs), 0)).astype(jnp.bfloat16)
    pair_doc = jnp.dot(own_doc, spread, preferred_element_type=jnp.float32).astype(jnp.int32)
    marks = pair_doc == lax.broadcasted_iota(jnp.int32, (docs, pairs), 0)
    low = lax.broadcasted_iota(jnp.int32, (docs, 128), 1) < 64
    step = 16
    for a in range(0, 64, step):
        block = jnp.broadcast_to(left[a:a + step][:, None, :], (step, docs, pairs))
        block = jnp.where(marks[None], block, 0.0).reshape(step * docs, pairs)
        got = jnp.dot(block.astype(jnp.bfloat16), right, preferred_element_type=jnp.float32)
        for j in range(0, step, 2):
            at = (a + j) * 64
            out_ref[:, at:at + 128] = jnp.where(
                low, got[j * docs:(j + 1) * docs], got[(j + 1) * docs:(j + 2) * docs])

    for make, conds in sent:
        when(conds, lambda: make().wait_send())


def shards(yn, tokens, grad_rows, routes, doc_ids, input_proj, grad_proj):
    tok, fan = routes.shape
    local, rank, width = input_proj.shape
    hidden = grad_proj.shape[2]
    zn = lax.axis_size("expert") // yn
    cols = local * rank
    pairs = tok * fan
    vmem = pl.BlockSpec(memory_space=pltpu.VMEM)
    hbm = pl.BlockSpec(memory_space=pl.ANY)
    dma = pltpu.SemaphoreType.DMA
    return pl.pallas_call(
        functools.partial(kernel, zn, yn, order_of(zn, yn)),
        out_shape=jax.ShapeDtypeStruct((DOC_DEV, rank * rank), jnp.float32),
        in_specs=[hbm, hbm, vmem, vmem, hbm, hbm],
        out_specs=vmem,
        scratch_shapes=[
            pltpu.VMEM((yn * tok, width), jnp.bfloat16),
            pltpu.VMEM((pairs, hidden), jnp.bfloat16),
            pltpu.VMEM((zn, cols, width), jnp.bfloat16),
            pltpu.VMEM((zn * yn, cols, hidden), jnp.bfloat16),
            pltpu.VMEM((zn, yn * tok, cols), jnp.bfloat16),
            pltpu.VMEM((zn, tok, cols), jnp.bfloat16),
            pltpu.VMEM((pairs, 128), jnp.float32),
            pltpu.VMEM((pairs, 128), jnp.float32),
            pltpu.VMEM((pairs, 128), jnp.int32),
            dma((4,)),
            dma((zn, 4)),
            dma((zn * yn, 4)),
            dma((4, zn, 2)),
            dma((5, zn * yn, 2)),
            dma,
            dma,
            dma((zn,)),
            dma((zn,)),
        ],
        compiler_params=pltpu.CompilerParams(
            collective_id=0, has_side_effects=True, vmem_limit_bytes=56 * 2**20),
        cost_estimate=pl.CostEstimate(
            flops=2 * pairs * hidden * cols * zn * yn + 2 * tok * yn * width * cols * zn,
            bytes_accessed=16 * 2**20, transcendentals=0),
        name="project_and_sum",
    )(tokens, grad_rows.reshape(pairs, hidden), routes, doc_ids.reshape(1, tok),
      input_proj.reshape(cols, width), grad_proj.reshape(cols, hidden))


def solution(mesh):
    in_specs = (
        P(("groups", "expert", "dp"), None),
        P(("groups", "expert", "dp"), None, None),
        P(("groups", "expert", "dp"), None),
        P(("groups", "expert", "dp")),
        P("expert", None, None),
        P("expert", None, None),
    )
    out_specs = P(("groups", "expert", "dp"), None)
    yn = 2 if mesh.shape["expert"] == 8 else 1
    return jax.shard_map(functools.partial(shards, yn), mesh=mesh, in_specs=in_specs,
                         out_specs=out_specs, check_vma=False)
```

```python
import functools

import jax
import jax.numpy as jnp
from jax import lax
from jax.experimental import pallas as pl
from jax.experimental.pallas import tpu as pltpu
from jax.sharding import PartitionSpec as P

DOC_DEV = 8
MESH = pl.DeviceIdType.MESH
LO, HI, XP, CORE, YP = range(5)
NT = (((1,), (1,)), ((), ()))
FULL_IN = ((3,), (1, 3))
FULL_GR = ()
FULL_Y = (0, 2)
FIRST_Z = ("gr", "ia", "ib")
FIRST_Y = ("tok", "g0", "g1")


def order_of(zn, yn):
    if (zn, yn) == (4, 2):
        return ORDER
    order = [("K", "gr", 0, 1, 0), ("T", 0, 1)]
    if yn == 2:
        order += [("Y", 0, 1), ("K", "gr", 0, 1, 1)]
    for d in range(1, zn):
        for s in (1, -1):
            order += [("Z", "gr", d, s), ("Z", "ia", d, s), ("Z", "ib", d, s)]
        for s in (1, -1):
            order += [("X", "gr", d, s, 0), ("X", "ia", d, s, 0), ("X", "ib", d, s, 0)]
            if yn == 2:
                order += [("Y", d, s), ("X", "gr", d, s, 1)]
        for s in (1, -1):
            order += [("K", "gr", d, s, 0), ("K", "in", d, s, 0)]
            if yn == 2:
                order += [("K", "gr", d, s, 1)]
    if yn == 2:
        order += [("F", d, s) for d in range(zn) for s in ((1, -1) if d else (1,))]
    return order


ORDER = [
    ("Z", "gr", 1, -1), ("Z", "gr", 1, 1), ("Z", "ia", 1, 1), ("Z", "ib", 1, 1), ("Z", "ia", 1, -1),
    ("T", 0, 1), ("X", "gr", 1, -1, 0), ("Z", "ib", 1, -1), ("Z", "gr", 2, -1), ("Z", "ia", 2, -1),
    ("X", "ia", 1, 1, 0), ("Z", "gr", 2, 1), ("X", "gr", 2, -1, 0), ("Z", "ib", 2, -1),
    ("X", "ib", 3, -1, 0), ("Y", 0, 1), ("X", "gr", 2, 1, 1), ("Z", "ia", 2, 1),
    ("K", "gr", 1, -1, 0), ("K", "gr", 0, 1, 0), ("X", "ia", 3, 1, 0), ("Z", "gr", 3, -1),
    ("K", "gr", 0, 1, 1), ("Y", 1, -1), ("Z", "ib", 2, 1), ("X", "ib", 2, -1, 0),
    ("X", "gr", 2, -1, 1), ("Z", "gr", 3, 1), ("X", "ia", 2, -1, 0), ("X", "gr", 1, 1, 0),
    ("X", "ia", 1, -1, 0), ("Y", 1, 1), ("X", "gr", 2, 1, 0), ("K", "in", 1, -1, 0),
    ("X", "gr", 3, -1, 0), ("K", "in", 1, 1, 0), ("F", 0, 1), ("X", "gr", 3, 1, 0),
    ("K", "gr", 2, -1, 0), ("K", "gr", 2, 1, 0), ("Y", 3, 1), ("X", "ia", 2, 1, 0),
    ("X", "ib", 2, 1, 0), ("Y", 3, -1), ("K", "gr", 1, 1, 0), ("K", "in", 2, 1, 0),
    ("X", "gr", 1, 1, 1), ("Z", "ia", 3, 1), ("Y", 2, 1), ("X", "gr", 1, -1, 1),
    ("K", "gr", 2, 1, 1), ("Z", "ib", 3, 1), ("X", "ib", 1, 1, 0), ("K", "in", 2, -1, 0),
    ("Y", 2, -1), ("Z", "ib", 3, -1), ("K", "gr", 1, -1, 1), ("X", "ia", 3, -1, 0), ("F", 1, 1),
    ("F", 1, -1), ("K", "in", 3, 1, 0), ("K", "gr", 3, -1, 0), ("K", "gr", 3, 1, 0),
    ("X", "ib", 1, -1, 0), ("Z", "ia", 3, -1), ("K", "gr", 2, -1, 1), ("X", "gr", 3, 1, 1),
    ("K", "in", 3, -1, 0), ("F", 2, 1), ("K", "gr", 1, 1, 1), ("F", 2, -1), ("X", "gr", 3, -1, 1),
    ("K", "gr", 3, -1, 1), ("K", "gr", 3, 1, 1), ("F", 3, 1), ("F", 3, -1), ("X", "ib", 3, 1, 0),
]


def kernel(zn, yn, order, tok_hbm, grad_hbm, routes_ref, doc_ref, win_hbm, wgr_hbm, out_ref,
           tok, grads, win, wgr, feat_send, feat_recv, acc_in, acc_gr, route_at,
           local_sem, in_recv, gr_recv, in_send, gr_send,
           tok_send_sem, tok_recv_sem, feat_send_sem, feat_recv_sem):
    group = lax.axis_index("groups")
    place = lax.axis_index("expert")
    core = lax.axis_index("dp")
    z, y = place // yn, place % yn
    hx = group % 2
    tokens = tok_hbm.shape[0]
    pairs = grad_hbm.shape[0]
    cols = win.shape[1]
    part = cols // 4
    size = {"gr": part, "ia": part // 2, "ib": part // 2}
    skip = {"gr": 0, "ia": 0, "ib": part // 2}
    last = zn - 1
    to = {
        LO: {"expert": place - yn},
        HI: {"expert": place + yn},
        XP: {"groups": group + 1 - 2 * hx},
        CORE: {"dp": 1 - core},
    }
    if yn == 2:
        to[YP] = {"expert": place + 1 - 2 * y}

    def have(link):
        if link == LO:
            return z > 0
        if link == HI:
            return z < last
        return None

    def when(conds, fn):
        conds = [c for c in conds if c is not None]
        if not conds:
            fn()
            return
        both = conds[0]
        for c in conds[1:]:
            both = jnp.logical_and(both, c)
        pl.when(both)(fn)

    def valid(d, sign):
        if d == 0:
            return None
        return z + d <= last if sign > 0 else z - d >= 0

    slot_own = z * yn + y
    local = [
        pltpu.make_async_copy(tok_hbm, tok.at[pl.ds(0, tokens)], local_sem.at[0]),
        pltpu.make_async_copy(wgr_hbm, wgr.at[slot_own], local_sem.at[1]),
        pltpu.make_async_copy(grad_hbm, grads, local_sem.at[2]),
        pltpu.make_async_copy(win_hbm, win.at[z], local_sem.at[3]),
    ]
    for c in local:
        c.start()

    barrier = pltpu.get_barrier_semaphore()
    for link in to:
        def greet(link=link):
            pl.semaphore_signal(barrier, inc=1, device_id=to[link], device_id_type=MESH)
        when([have(link)], greet)
    inner = (z > 0).astype(jnp.int32) + (z < last).astype(jnp.int32)
    pl.semaphore_wait(barrier, len(to) - 2 + inner)

    sent = []

    def send(make, conds):
        when(conds, lambda: make().start())
        sent.append((make, conds))

    def rows_of(kind, dh, dc=0):
        half = hx if dh == 0 else 1 - hx
        which = core if dc == 0 else 1 - core
        number = half * 2 + which
        start = pl.multiple_of(number * part + skip[kind], part // 2)
        if kind == "ib":
            number += 4
        return pl.ds(start, size[kind]), number

    def pack(kind, d, sign, yr):
        zz = z + sign * d
        if kind != "gr":
            return win, zz, in_send, in_recv
        yy = y if yr == 0 else 1 - y
        return wgr, zz * yn + yy, gr_send, gr_recv

    def send_piece(kind, d, sign, yr, dh, link):
        buf, slot, ssem, rsem = pack(kind, d, sign, yr)
        rows, number = rows_of(kind, dh)
        if d == 0 and yr == 0:
            src = (wgr_hbm if kind == "gr" else win_hbm).at[rows]
        else:
            src = buf.at[slot, rows]

        def make():
            return pltpu.make_async_remote_copy(
                src_ref=src, dst_ref=buf.at[slot, rows],
                send_sem=ssem.at[link, slot, dh + 2 * (kind == "ib")], recv_sem=rsem.at[slot, number],
                device_id=to[link], device_id_type=MESH)
        send(make, [valid(d, sign), have(link)])

    def arrive(kind, d, sign, yr, dh, dc=0):
        buf, slot, ssem, rsem = pack(kind, d, sign, yr)
        rows, number = rows_of(kind, dh, dc)

        def wait():
            pltpu.make_async_remote_copy(
                src_ref=buf.at[slot, rows], dst_ref=buf.at[slot, rows],
                send_sem=ssem.at[CORE, slot, dh], recv_sem=rsem.at[slot, number],
                device_id=to[CORE], device_id_type=MESH).wait_recv()
        when([valid(d, sign)], wait)

    full_z = {"ia": FULL_IN[0], "ib": FULL_IN[1], "gr": FULL_GR}

    def z_event(kind, d, sign):
        link = LO if sign > 0 else HI
        full = d in full_z[kind]
        arrive(kind, d, sign, 0, 0)
        if d < last:
            send_piece(kind, d, sign, 0, 0, link)
        if kind == "gr" and yn == 2:
            send_piece(kind, d, sign, 0, 0, YP)
        if not full:
            send_piece(kind, d, sign, 0, 0, XP)
        send_piece(kind, d, sign, 0, 0, CORE)
        if full:
            arrive(kind, d, sign, 0, 1)
            other_half(kind, d, sign)

    def other_half(kind, d, sign):
        if d < last and d + 1 in full_z[kind]:
            send_piece(kind, d, sign, 0, 1, LO if sign > 0 else HI)
        if kind == "gr" and yn == 2 and d in FULL_Y:
            send_piece(kind, d, sign, 0, 1, YP)
        send_piece(kind, d, sign, 0, 1, CORE)

    def y_event(d, sign):
        arrive("gr", d, sign, 1, 0)
        if d not in FULL_Y:
            send_piece("gr", d, sign, 1, 0, XP)
        send_piece("gr", d, sign, 1, 0, CORE)
        if d in FULL_Y:
            arrive("gr", d, sign, 1, 1)
            send_piece("gr", d, sign, 1, 1, CORE)

    def x_event(kind, d, sign, yr):
        if d in (full_z[kind] if yr == 0 else FULL_Y):
            return
        arrive(kind, d, sign, yr, 1)
        if yr == 0:
            other_half(kind, d, sign)
        else:
            send_piece(kind, d, sign, yr, 1, CORE)

    def core_event(kind, d, sign, yr):
        for piece in ("gr",) if kind == "gr" else ("ia", "ib"):
            arrive(piece, d, sign, yr, 0, 1)
            arrive(piece, d, sign, yr, 1, 1)

    tile = 256

    def select(acc, at, slot, value):
        hit = route_at[pl.ds(at, tile), :]
        acc[pl.ds(at, tile), :] = jnp.where(
            hit == 4 * slot, value[:, :128],
            jnp.where(hit == 4 * slot + 2, value[:, 128:], acc[pl.ds(at, tile), :]))

    def project_grads(d, sign, yr):
        _, slot, _, _ = pack("gr", d, sign, yr)

        def run():
            @pl.loop(0, pairs // tile)
            def _(i):
                at = pl.multiple_of(i * tile, tile)
                value = lax.dot_general(grads[pl.ds(at, tile), :], wgr[slot], NT,
                                        preferred_element_type=jnp.float32)
                select(acc_gr, at, slot, value)
        when([valid(d, sign)], run)

    fan = pairs // tokens

    def select_inputs(slot, block):
        @pl.loop(0, pairs // tile)
        def _(i):
            at = pl.multiple_of(i * tile, tile)
            few = tile // fan
            value = block[pl.ds(pl.multiple_of(i * few, few), few), :].astype(jnp.float32)
            value = jnp.broadcast_to(value[:, None, :], (few, fan, cols)).reshape(tile, cols)
            select(acc_in, at, slot, value)

    def project_inputs(d, sign):
        _, slot, _, _ = pack("ia", d, sign, 0)

        def run():
            value = lax.dot_general(tok[...], win[slot], NT, preferred_element_type=jnp.float32)
            feat_send[slot] = value.astype(jnp.bfloat16)
        when([valid(d, sign)], run)
        if yn == 2:
            def make():
                return pltpu.make_async_remote_copy(
                    src_ref=feat_send.at[slot, pl.ds(tokens, tokens)], dst_ref=feat_recv.at[slot],
                    send_sem=feat_send_sem.at[slot], recv_sem=feat_recv_sem.at[slot],
                    device_id=to[YP], device_id_type=MESH)
            send(make, [valid(d, sign)])
        when([valid(d, sign)], lambda: select_inputs(slot * yn + y, feat_send.at[slot]))

    def features_back(d, sign):
        if yn == 1:
            return
        _, slot, _, _ = pack("ia", d, sign, 0)

        def run():
            pltpu.make_async_remote_copy(
                src_ref=feat_recv.at[slot], dst_ref=feat_recv.at[slot],
                send_sem=feat_send_sem.at[slot], recv_sem=feat_recv_sem.at[slot],
                device_id=to[YP], device_id_type=MESH).wait_recv()
            select_inputs(slot * yn + 1 - y, feat_recv.at[slot])
        when([valid(d, sign)], run)

    def make_tok():
        return pltpu.make_async_remote_copy(
            src_ref=tok_hbm, dst_ref=tok.at[pl.ds(tokens, tokens)],
            send_sem=tok_send_sem, recv_sem=tok_recv_sem,
            device_id=to[YP], device_id_type=MESH)

    for kind in FIRST_Z:
        for link in (LO, HI):
            send_piece(kind, 0, 1, 0, 0, link)
            if 1 in full_z[kind]:
                send_piece(kind, 0, 1, 0, 1, link)
    if yn == 2:
        for what in FIRST_Y:
            if what == "tok":
                send(make_tok, [])
                continue
            if what == "g0":
                send_piece("gr", 0, 1, 0, 0, YP)
            elif 0 in FULL_Y:
                send_piece("gr", 0, 1, 0, 1, YP)

    pair = lax.broadcasted_iota(jnp.int32, (pairs, tokens), 0) // fan
    spread = (pair == lax.broadcasted_iota(jnp.int32, (pairs, tokens), 1)).astype(jnp.bfloat16)
    named = lax.dot_general(spread, routes_ref[...].astype(jnp.bfloat16), NT,
                            preferred_element_type=jnp.float32)
    choice = lax.broadcasted_iota(jnp.int32, (pairs, fan), 0) % fan
    mine = choice == lax.broadcasted_iota(jnp.int32, (pairs, fan), 1)
    named = jnp.sum(jnp.where(mine, named, 0.0), axis=1, keepdims=True).astype(jnp.int32)
    half_of = lax.broadcasted_iota(jnp.int32, (pairs, 128), 1) // 64
    route_at[...] = named - half_of
    acc_in[...] = jnp.zeros_like(acc_in)
    acc_gr[...] = jnp.zeros_like(acc_gr)
    for c in local:
        c.wait()

    def run_event(event):
        what = event[0]
        if what == "Z":
            z_event(*event[1:])
        elif what == "X":
            x_event(*event[1:])
        elif what == "Y":
            y_event(*event[1:])
        elif what == "F":
            features_back(*event[1:])
        elif what == "T":
            if yn == 2:
                make_tok().wait_recv()
            project_inputs(0, 1)
        else:
            kind, d, sign, yr = event[1:]
            if (d, yr) != (0, 0):
                core_event(kind, d, sign, yr)
            if kind == "in":
                project_inputs(d, sign)
            else:
                project_grads(d, sign, yr)

    for event in order:
        run_event(event)

    right = acc_in[...]
    right = (right + pltpu.roll(right, 64, 1)).astype(jnp.bfloat16)
    left = acc_gr[...]
    left = (left + pltpu.roll(left, 64, 1)).astype(jnp.bfloat16).astype(jnp.float32)
    left = left.T
    docs = out_ref.shape[0]
    first = (place * lax.axis_size("dp") + core) * docs
    own_doc = jnp.broadcast_to(doc_ref[...] - first, (docs, tokens)).astype(jnp.bfloat16)
    pair = lax.broadcasted_iota(jnp.int32, (tokens, pairs), 1) // fan
    spread = (pair == lax.broadcasted_iota(jnp.int32, (tokens, pairs), 0)).astype(jnp.bfloat16)
    pair_doc = jnp.dot(own_doc, spread, preferred_element_type=jnp.float32).astype(jnp.int32)
    marks = pair_doc == lax.broadcasted_iota(jnp.int32, (docs, pairs), 0)
    low = lax.broadcasted_iota(jnp.int32, (docs, 128), 1) < 64
    step = 16
    for a in range(0, 64, step):
        block = jnp.broadcast_to(left[a:a + step][:, None, :], (step, docs, pairs))
        block = jnp.where(marks[None], block, 0.0).reshape(step * docs, pairs)
        got = jnp.dot(block.astype(jnp.bfloat16), right, preferred_element_type=jnp.float32)
        for j in range(0, step, 2):
            at = (a + j) * 64
            out_ref[:, at:at + 128] = jnp.where(
                low, got[j * docs:(j + 1) * docs], got[(j + 1) * docs:(j + 2) * docs])

    for make, conds in sent:
        when(conds, lambda: make().wait_send())


def shards(yn, tokens, grad_rows, routes, doc_ids, input_proj, grad_proj):
    tok, fan = routes.shape
    local, rank, width = input_proj.shape
    hidden = grad_proj.shape[2]
    zn = lax.axis_size("expert") // yn
    cols = local * rank
    pairs = tok * fan
    vmem = pl.BlockSpec(memory_space=pltpu.VMEM)
    hbm = pl.BlockSpec(memory_space=pl.ANY)
    dma = pltpu.SemaphoreType.DMA
    return pl.pallas_call(
        functools.partial(kernel, zn, yn, order_of(zn, yn)),
        out_shape=jax.ShapeDtypeStruct((DOC_DEV, rank * rank), jnp.float32),
        in_specs=[hbm, hbm, vmem, vmem, hbm, hbm],
        out_specs=vmem,
        scratch_shapes=[
            pltpu.VMEM((yn * tok, width), jnp.bfloat16),
            pltpu.VMEM((pairs, hidden), jnp.bfloat16),
            pltpu.VMEM((zn, cols, width), jnp.bfloat16),
            pltpu.VMEM((zn * yn, cols, hidden), jnp.bfloat16),
            pltpu.VMEM((zn, yn * tok, cols), jnp.bfloat16),
            pltpu.VMEM((zn, tok, cols), jnp.bfloat16),
            pltpu.VMEM((pairs, 128), jnp.float32),
            pltpu.VMEM((pairs, 128), jnp.float32),
            pltpu.VMEM((pairs, 128), jnp.int32),
            dma((4,)),
            dma((zn, 8)),
            dma((zn * yn, 4)),
            dma((4, zn, 4)),
            dma((5, zn * yn, 2)),
            dma,
            dma,
            dma((zn,)),
            dma((zn,)),
        ],
        compiler_params=pltpu.CompilerParams(
            collective_id=0, has_side_effects=True, vmem_limit_bytes=56 * 2**20),
        cost_estimate=pl.CostEstimate(
            flops=2 * pairs * hidden * cols * zn * yn + 2 * tok * yn * width * cols * zn,
            bytes_accessed=16 * 2**20, transcendentals=0),
        name="project_and_sum",
    )(tokens, grad_rows.reshape(pairs, hidden), routes.T, doc_ids.reshape(1, tok),
      input_proj.reshape(cols, width), grad_proj.reshape(cols, hidden))


def solution(mesh):
    in_specs = (
        P(("groups", "expert", "dp"), None),
        P(("groups", "expert", "dp"), None, None),
        P(("groups", "expert", "dp"), None),
        P(("groups", "expert", "dp")),
        P("expert", None, None),
        P("expert", None, None),
    )
    out_specs = P(("groups", "expert", "dp"), None)
    yn = 2 if mesh.shape["expert"] == 8 else 1
    return jax.shard_map(functools.partial(shards, yn), mesh=mesh, in_specs=in_specs,
                         out_specs=out_specs, check_vma=False)
```

```python
import functools

import jax
import jax.numpy as jnp
from jax import lax
from jax.experimental import pallas as pl
from jax.experimental.pallas import tpu as pltpu
from jax.sharding import PartitionSpec as P

DOC_DEV = 8
MESH = pl.DeviceIdType.MESH
LO, HI, XP, CORE, YP = range(5)
NT = (((1,), (1,)), ((), ()))
FULL_IN = (3,)
FULL_GR = (1,)
FULL_Y = (0, 1)
FIRST_Z = ("in", "gr")
FIRST_Y = ("gr", "tok")


def order_of(zn, yn):
    if (zn, yn) == (4, 2):
        return ORDER
    order = [("K", "gr", 0, 1, 0), ("T", 0, 1)]
    if yn == 2:
        order += [("Y", 0, 1), ("K", "gr", 0, 1, 1)]
    for d in range(1, zn):
        for s in (1, -1):
            order += [("Z", "gr", d, s), ("Z", "in", d, s)]
        for s in (1, -1):
            order += [("X", "gr", d, s, 0), ("X", "in", d, s, 0)]
            if yn == 2:
                order += [("Y", d, s), ("X", "gr", d, s, 1)]
        for s in (1, -1):
            order += [("K", "gr", d, s, 0), ("K", "in", d, s, 0)]
            if yn == 2:
                order += [("K", "gr", d, s, 1)]
    if yn == 2:
        order += [("F", d, s) for d in range(zn) for s in ((1, -1) if d else (1,))]
    return order


ORDER = [
    ("Y", 0, 1), ("X", "gr", 1, 1, 1), ("Z", "in", 1, 1), ("Z", "gr", 1, -1), ("Z", "in", 1, -1),
    ("Z", "gr", 2, -1), ("K", "gr", 1, -1, 0), ("Z", "gr", 1, 1), ("X", "in", 3, -1, 0),
    ("K", "gr", 0, 1, 1), ("X", "in", 1, 1, 0), ("X", "in", 3, 1, 0), ("Z", "in", 2, 1),
    ("X", "gr", 2, -1, 0), ("Z", "gr", 2, 1), ("Z", "in", 2, -1), ("T", 0, 1), ("Y", 1, -1),
    ("K", "in", 1, 1, 0), ("K", "gr", 1, -1, 1), ("X", "in", 2, 1, 0), ("X", "gr", 1, -1, 0),
    ("K", "gr", 2, -1, 0), ("Y", 2, -1), ("X", "in", 2, -1, 0), ("Z", "gr", 3, -1),
    ("X", "in", 1, -1, 0), ("K", "gr", 0, 1, 0), ("X", "gr", 2, -1, 1), ("K", "in", 2, -1, 0),
    ("K", "gr", 1, 1, 0), ("Y", 2, 1), ("Z", "gr", 3, 1), ("Y", 3, -1), ("Y", 1, 1),
    ("K", "in", 1, -1, 0), ("F", 0, 1), ("K", "in", 2, 1, 0), ("Z", "in", 3, -1), ("F", 2, -1),
    ("X", "gr", 3, -1, 0), ("K", "gr", 2, -1, 1), ("X", "gr", 2, 1, 1), ("K", "gr", 1, 1, 1),
    ("F", 1, -1), ("Y", 3, 1), ("K", "in", 3, -1, 0), ("K", "gr", 2, 1, 1), ("Z", "in", 3, 1),
    ("F", 1, 1), ("X", "gr", 1, 1, 0), ("X", "gr", 3, -1, 1), ("X", "gr", 1, -1, 1),
    ("K", "gr", 3, -1, 0), ("X", "gr", 2, 1, 0), ("K", "gr", 3, -1, 1), ("X", "gr", 3, 1, 0),
    ("F", 2, 1), ("K", "in", 3, 1, 0), ("K", "gr", 2, 1, 0), ("X", "gr", 3, 1, 1),
    ("K", "gr", 3, 1, 0), ("K", "gr", 3, 1, 1), ("F", 3, 1), ("F", 3, -1),
]


def kernel(zn, yn, order, tok_hbm, grad_hbm, routes_ref, doc_ref, win_hbm, wgr_hbm, out_ref,
           tok, grads, win, wgr, feat_send, feat_recv, acc_in, acc_gr, route_at,
           local_sem, in_recv, gr_recv, in_send, gr_send,
           tok_send_sem, tok_recv_sem, feat_send_sem, feat_recv_sem):
    group = lax.axis_index("groups")
    place = lax.axis_index("expert")
    core = lax.axis_index("dp")
    z, y = place // yn, place % yn
    hx = group % 2
    tokens = tok_hbm.shape[0]
    pairs = grad_hbm.shape[0]
    cols = win.shape[1]
    part = cols // 4
    last = zn - 1
    to = {
        LO: {"expert": place - yn},
        HI: {"expert": place + yn},
        XP: {"groups": group + 1 - 2 * hx},
        CORE: {"dp": 1 - core},
    }
    if yn == 2:
        to[YP] = {"expert": place + 1 - 2 * y}

    def have(link):
        if link == LO:
            return z > 0
        if link == HI:
            return z < last
        return None

    def when(conds, fn):
        conds = [c for c in conds if c is not None]
        if not conds:
            fn()
            return
        both = conds[0]
        for c in conds[1:]:
            both = jnp.logical_and(both, c)
        pl.when(both)(fn)

    def valid(d, sign):
        if d == 0:
            return None
        return z + d <= last if sign > 0 else z - d >= 0

    slot_own = z * yn + y
    local = [
        pltpu.make_async_copy(tok_hbm, tok.at[pl.ds(0, tokens)], local_sem.at[0]),
        pltpu.make_async_copy(wgr_hbm, wgr.at[slot_own], local_sem.at[1]),
        pltpu.make_async_copy(grad_hbm, grads, local_sem.at[2]),
        pltpu.make_async_copy(win_hbm, win.at[z], local_sem.at[3]),
    ]
    for c in local:
        c.start()

    barrier = pltpu.get_barrier_semaphore()
    for link in to:
        def greet(link=link):
            pl.semaphore_signal(barrier, inc=1, device_id=to[link], device_id_type=MESH)
        when([have(link)], greet)
    inner = (z > 0).astype(jnp.int32) + (z < last).astype(jnp.int32)
    pl.semaphore_wait(barrier, len(to) - 2 + inner)

    sent = []

    def send(make, conds):
        when(conds, lambda: make().start())
        sent.append((make, conds))

    def rows_of(dh, dc=0):
        half = hx if dh == 0 else 1 - hx
        which = core if dc == 0 else 1 - core
        return pl.ds(pl.multiple_of((half * 2 + which) * part, part), part), half * 2 + which

    def pack(kind, d, sign, yr):
        zz = z + sign * d
        if kind == "in":
            return win, zz, in_send, in_recv
        yy = y if yr == 0 else 1 - y
        return wgr, zz * yn + yy, gr_send, gr_recv

    def send_piece(kind, d, sign, yr, dh, link):
        buf, slot, ssem, rsem = pack(kind, d, sign, yr)
        rows, number = rows_of(dh)
        if d == 0 and yr == 0:
            src = (win_hbm if kind == "in" else wgr_hbm).at[rows]
        else:
            src = buf.at[slot, rows]

        def make():
            return pltpu.make_async_remote_copy(
                src_ref=src, dst_ref=buf.at[slot, rows],
                send_sem=ssem.at[link, slot, dh], recv_sem=rsem.at[slot, number],
                device_id=to[link], device_id_type=MESH)
        send(make, [valid(d, sign), have(link)])

    def arrive(kind, d, sign, yr, dh, dc=0):
        buf, slot, ssem, rsem = pack(kind, d, sign, yr)
        rows, number = rows_of(dh, dc)

        def wait():
            pltpu.make_async_remote_copy(
                src_ref=buf.at[slot, rows], dst_ref=buf.at[slot, rows],
                send_sem=ssem.at[CORE, slot, dh], recv_sem=rsem.at[slot, number],
                device_id=to[CORE], device_id_type=MESH).wait_recv()
        when([valid(d, sign)], wait)

    full_z = {"in": FULL_IN, "gr": FULL_GR}

    def z_event(kind, d, sign):
        link = LO if sign > 0 else HI
        full = d in full_z[kind]
        arrive(kind, d, sign, 0, 0)
        if d < last:
            send_piece(kind, d, sign, 0, 0, link)
        if kind == "gr" and yn == 2:
            send_piece(kind, d, sign, 0, 0, YP)
        if not full:
            send_piece(kind, d, sign, 0, 0, XP)
        send_piece(kind, d, sign, 0, 0, CORE)
        if full:
            arrive(kind, d, sign, 0, 1)
            other_half(kind, d, sign)

    def other_half(kind, d, sign):
        if d < last and d + 1 in full_z[kind]:
            send_piece(kind, d, sign, 0, 1, LO if sign > 0 else HI)
        if kind == "gr" and yn == 2 and d in FULL_Y:
            send_piece(kind, d, sign, 0, 1, YP)
        send_piece(kind, d, sign, 0, 1, CORE)

    def y_event(d, sign):
        arrive("gr", d, sign, 1, 0)
        if d not in FULL_Y:
            send_piece("gr", d, sign, 1, 0, XP)
        send_piece("gr", d, sign, 1, 0, CORE)
        if d in FULL_Y:
            arrive("gr", d, sign, 1, 1)
            send_piece("gr", d, sign, 1, 1, CORE)

    def x_event(kind, d, sign, yr):
        if d in (full_z[kind] if yr == 0 else FULL_Y):
            return
        arrive(kind, d, sign, yr, 1)
        if yr == 0:
            other_half(kind, d, sign)
        else:
            send_piece(kind, d, sign, yr, 1, CORE)

    def core_event(kind, d, sign, yr):
        arrive(kind, d, sign, yr, 0, 1)
        arrive(kind, d, sign, yr, 1, 1)

    tile = 256

    def select(acc, at, slot, value):
        hit = route_at[pl.ds(at, tile), :]
        acc[pl.ds(at, tile), :] = jnp.where(
            hit == 4 * slot, value[:, :128],
            jnp.where(hit == 4 * slot + 2, value[:, 128:], acc[pl.ds(at, tile), :]))

    def project_grads(d, sign, yr):
        _, slot, _, _ = pack("gr", d, sign, yr)

        def run():
            @pl.loop(0, pairs // tile)
            def _(i):
                at = pl.multiple_of(i * tile, tile)
                value = lax.dot_general(grads[pl.ds(at, tile), :], wgr[slot], NT,
                                        preferred_element_type=jnp.float32)
                select(acc_gr, at, slot, value)
        when([valid(d, sign)], run)

    fan = pairs // tokens

    def select_inputs(slot, block):
        @pl.loop(0, pairs // tile)
        def _(i):
            at = pl.multiple_of(i * tile, tile)
            few = tile // fan
            value = block[pl.ds(pl.multiple_of(i * few, few), few), :].astype(jnp.float32)
            value = jnp.broadcast_to(value[:, None, :], (few, fan, cols)).reshape(tile, cols)
            select(acc_in, at, slot, value)

    def project_inputs(d, sign):
        _, slot, _, _ = pack("in", d, sign, 0)

        def run():
            value = lax.dot_general(tok[...], win[slot], NT, preferred_element_type=jnp.float32)
            feat_send[slot] = value.astype(jnp.bfloat16)
        when([valid(d, sign)], run)
        if yn == 2:
            def make():
                return pltpu.make_async_remote_copy(
                    src_ref=feat_send.at[slot, pl.ds(tokens, tokens)], dst_ref=feat_recv.at[slot],
                    send_sem=feat_send_sem.at[slot], recv_sem=feat_recv_sem.at[slot],
                    device_id=to[YP], device_id_type=MESH)
            send(make, [valid(d, sign)])
        when([valid(d, sign)], lambda: select_inputs(slot * yn + y, feat_send.at[slot]))

    def features_back(d, sign):
        if yn == 1:
            return
        _, slot, _, _ = pack("in", d, sign, 0)

        def run():
            pltpu.make_async_remote_copy(
                src_ref=feat_recv.at[slot], dst_ref=feat_recv.at[slot],
                send_sem=feat_send_sem.at[slot], recv_sem=feat_recv_sem.at[slot],
                device_id=to[YP], device_id_type=MESH).wait_recv()
            select_inputs(slot * yn + 1 - y, feat_recv.at[slot])
        when([valid(d, sign)], run)

    def make_tok():
        return pltpu.make_async_remote_copy(
            src_ref=tok_hbm, dst_ref=tok.at[pl.ds(tokens, tokens)],
            send_sem=tok_send_sem, recv_sem=tok_recv_sem,
            device_id=to[YP], device_id_type=MESH)

    for kind in FIRST_Z:
        for link in (LO, HI):
            send_piece(kind, 0, 1, 0, 0, link)
            if 1 in full_z[kind]:
                send_piece(kind, 0, 1, 0, 1, link)
    if yn == 2:
        for what in FIRST_Y:
            if what == "tok":
                send(make_tok, [])
                continue
            send_piece("gr", 0, 1, 0, 0, YP)
            if 0 in FULL_Y:
                send_piece("gr", 0, 1, 0, 1, YP)

    pair = lax.broadcasted_iota(jnp.int32, (pairs, tokens), 0) // fan
    spread = (pair == lax.broadcasted_iota(jnp.int32, (pairs, tokens), 1)).astype(jnp.bfloat16)
    named = lax.dot_general(spread, routes_ref[...].astype(jnp.bfloat16), NT,
                            preferred_element_type=jnp.float32)
    choice = lax.broadcasted_iota(jnp.int32, (pairs, fan), 0) % fan
    mine = choice == lax.broadcasted_iota(jnp.int32, (pairs, fan), 1)
    named = jnp.sum(jnp.where(mine, named, 0.0), axis=1, keepdims=True).astype(jnp.int32)
    half_of = lax.broadcasted_iota(jnp.int32, (pairs, 128), 1) // 64
    route_at[...] = named - half_of
    acc_in[...] = jnp.zeros_like(acc_in)
    acc_gr[...] = jnp.zeros_like(acc_gr)
    for c in local:
        c.wait()

    def run_event(event):
        what = event[0]
        if what == "Z":
            z_event(*event[1:])
        elif what == "X":
            x_event(*event[1:])
        elif what == "Y":
            y_event(*event[1:])
        elif what == "F":
            features_back(*event[1:])
        elif what == "T":
            if yn == 2:
                make_tok().wait_recv()
            project_inputs(0, 1)
        else:
            kind, d, sign, yr = event[1:]
            if (d, yr) != (0, 0):
                core_event(kind, d, sign, yr)
            if kind == "in":
                project_inputs(d, sign)
            else:
                project_grads(d, sign, yr)

    for event in order:
        run_event(event)

    right = acc_in[...]
    right = (right + pltpu.roll(right, 64, 1)).astype(jnp.bfloat16)
    left = acc_gr[...]
    left = (left + pltpu.roll(left, 64, 1)).astype(jnp.bfloat16).astype(jnp.float32)
    left = left.T
    docs = out_ref.shape[0]
    first = (place * lax.axis_size("dp") + core) * docs
    own_doc = jnp.broadcast_to(doc_ref[...] - first, (docs, tokens)).astype(jnp.bfloat16)
    pair = lax.broadcasted_iota(jnp.int32, (tokens, pairs), 1) // fan
    spread = (pair == lax.broadcasted_iota(jnp.int32, (tokens, pairs), 0)).astype(jnp.bfloat16)
    pair_doc = jnp.dot(own_doc, spread, preferred_element_type=jnp.float32).astype(jnp.int32)
    marks = pair_doc == lax.broadcasted_iota(jnp.int32, (docs, pairs), 0)
    low = lax.broadcasted_iota(jnp.int32, (docs, 128), 1) < 64
    step = 16
    for a in range(0, 64, step):
        block = jnp.broadcast_to(left[a:a + step][:, None, :], (step, docs, pairs))
        block = jnp.where(marks[None], block, 0.0).reshape(step * docs, pairs)
        got = jnp.dot(block.astype(jnp.bfloat16), right, preferred_element_type=jnp.float32)
        for j in range(0, step, 2):
            at = (a + j) * 64
            out_ref[:, at:at + 128] = jnp.where(
                low, got[j * docs:(j + 1) * docs], got[(j + 1) * docs:(j + 2) * docs])

    for make, conds in sent:
        when(conds, lambda: make().wait_send())


def shards(yn, tokens, grad_rows, routes, doc_ids, input_proj, grad_proj):
    tok, fan = routes.shape
    local, rank, width = input_proj.shape
    hidden = grad_proj.shape[2]
    zn = lax.axis_size("expert") // yn
    cols = local * rank
    pairs = tok * fan
    vmem = pl.BlockSpec(memory_space=pltpu.VMEM)
    hbm = pl.BlockSpec(memory_space=pl.ANY)
    dma = pltpu.SemaphoreType.DMA
    return pl.pallas_call(
        functools.partial(kernel, zn, yn, order_of(zn, yn)),
        out_shape=jax.ShapeDtypeStruct((DOC_DEV, rank * rank), jnp.float32),
        in_specs=[hbm, hbm, vmem, vmem, hbm, hbm],
        out_specs=vmem,
        scratch_shapes=[
            pltpu.VMEM((yn * tok, width), jnp.bfloat16),
            pltpu.VMEM((pairs, hidden), jnp.bfloat16),
            pltpu.VMEM((zn, cols, width), jnp.bfloat16),
            pltpu.VMEM((zn * yn, cols, hidden), jnp.bfloat16),
            pltpu.VMEM((zn, yn * tok, cols), jnp.bfloat16),
            pltpu.VMEM((zn, tok, cols), jnp.bfloat16),
            pltpu.VMEM((pairs, 128), jnp.float32),
            pltpu.VMEM((pairs, 128), jnp.float32),
            pltpu.VMEM((pairs, 128), jnp.int32),
            dma((4,)),
            dma((zn, 4)),
            dma((zn * yn, 4)),
            dma((4, zn, 2)),
            dma((5, zn * yn, 2)),
            dma,
            dma,
            dma((zn,)),
            dma((zn,)),
        ],
        compiler_params=pltpu.CompilerParams(
            collective_id=0, has_side_effects=True, vmem_limit_bytes=56 * 2**20),
        cost_estimate=pl.CostEstimate(
            flops=2 * pairs * hidden * cols * zn * yn + 2 * tok * yn * width * cols * zn,
            bytes_accessed=16 * 2**20, transcendentals=0),
        name="project_and_sum",
    )(tokens, grad_rows.reshape(pairs, hidden), routes.T, doc_ids.reshape(1, tok),
      input_proj.reshape(cols, width), grad_proj.reshape(cols, hidden))


def solution(mesh):
    in_specs = (
        P(("groups", "expert", "dp"), None),
        P(("groups", "expert", "dp"), None, None),
        P(("groups", "expert", "dp"), None),
        P(("groups", "expert", "dp")),
        P("expert", None, None),
        P("expert", None, None),
    )
    out_specs = P(("groups", "expert", "dp"), None)
    yn = 2 if mesh.shape["expert"] == 8 else 1
    return jax.shard_map(functools.partial(shards, yn), mesh=mesh, in_specs=in_specs,
                         out_specs=out_specs, check_vma=False)
```
